32 devices in a mesh: band: 4 (over x, core), grid: 8 (over z, y).
Axes of the slice: x: 2, y: 2, z: 4, core: 2. Of those that a mesh axis runs over, the one named last changes fastest.
Arguments:
- targets: float32 [8, 128, 128, 128], P('band', 'grid'), may hold values from -6 to 6
- occupied: float32 [8, 128, 128, 128], P('band', 'grid'), may hold values from -6 to 6
- owners: int32 [2], replicated, may hold values from 0 to 7, as said below
- cutoff_mask: int32 [128, 128, 128], P(None, 'grid'), may hold values from 0 to 1, as said below
Outputs:
- exchange_applied: float32 [8, 128, 128, 128], P('band', 'grid')
The draws below stay inside these ranges and needn't reach their ends.
Inputs may be any that keep to these rules, and one draw needn't show every extreme that they name: `owners`: distinct; orbital 8 - 1 is always among them, in a slot that varies; occupied orbital o is stored by band group o // 2 in its slot o % 2. `cutoff_mask`: symmetric: the mask at k equals the mask at -k, indices taken modulo 128 along each dimension.
All inputs are finite; a program needn't handle non-finite values.
Results may differ from the reference program's by a relative error of at most 0.00012.
Values sent between devices are 32-bit elements; how exact they have to be, the bound alone decides.
A program may use at most 64 MiB of HBM per device.

```python
import jax
import jax.numpy as jnp
from jax import lax

NG = 128
OCC = 8
TARGETS = 8
WINDOW = 2


def draw_owners(key, part):
    key = jax.random.fold_in(key, 11)
    first_key, second_key = jax.random.split(key)
    others = jax.random.permutation(first_key, OCC - 1)[:WINDOW - 1].astype(jnp.int32)
    chosen = jnp.concatenate([others, jnp.full((1,), OCC - 1, jnp.int32)])
    order = jax.random.permutation(second_key, WINDOW)
    return chosen[order].astype(jnp.int32)


def draw_cutoff_mask(key, part):
    key = jax.random.fold_in(key, 23)
    raw_bits = jax.random.randint(key, (NG, NG, NG), 0, 4)
    chosen = (raw_bits > 0).astype(jnp.int32)
    mirror = jnp.roll(jnp.flip(chosen, (0, 1, 2)), 1, (0, 1, 2))
    return chosen * mirror


def block_scale(rng, extent, cuts, least, high):
    loudness = 1.0
    for dim, blocks in cuts:
        steps = jax.random.uniform(jax.random.fold_in(jax.random.fold_in(rng, 6), dim), (blocks,), jnp.float32, least / len(cuts), high / len(cuts))
        loudness = loudness * jnp.repeat(jnp.exp(steps), extent[dim] // blocks).reshape((-1,) + (1,) * (len(extent) - 1 - dim))
    return loudness


def gaussian(key, dims, width, limit, cuts=(), kind=jnp.bfloat16):
    drawn = jax.random.normal(key, dims, jnp.float32) * width
    if len(cuts) > 0:
        drawn = block_scale(key, dims, cuts, -0.22, 0.18) * drawn
    return jnp.clip(drawn, min=-limit, max=limit).astype(kind)


def setup_inputs(seed: int = 0) -> dict:
    keys = jax.random.split(jax.random.key(seed), 5)
    targets = gaussian(keys[0], (TARGETS, NG, NG, NG), 1.0, 6.0, ((0, 4), (1, 8)), jnp.float32)
    occupied = gaussian(keys[1], (OCC, NG, NG, NG), 1.0, 6.0, ((0, 4), (1, 8)), jnp.float32)
    owners = draw_owners(jax.random.fold_in(keys[4], 71), 0)
    cutoff_mask = draw_cutoff_mask(jax.random.fold_in(keys[4], 71), 0)
    return {"targets": targets, "occupied": occupied, "owners": owners, "cutoff_mask": cutoff_mask}


screen = 1600.0


def frequencies(count):
    index = jnp.arange(count, dtype=jnp.int32)
    return jnp.where(index < count // 2, index, index - count).astype(jnp.float32)


def reference(targets, occupied, owners, cutoff_mask):
    freq = frequencies(NG)
    squared = freq[:, None, None] ** 2 + freq[None, :, None] ** 2 + freq[None, None, :] ** 2
    coulomb = screen / (screen + squared) * cutoff_mask.astype(jnp.float32)

    def apply_one(target):
        total = jnp.zeros(target.shape, jnp.float32)
        for position in range(WINDOW):
            orbital = occupied[owners[position]]
            spectrum = jnp.fft.fftn(orbital * target) * coulomb
            potential = jnp.real(jnp.fft.ifftn(spectrum))
            total = total + orbital * potential
        return -total

    return lax.map(apply_one, targets)
```

```python
import math

import jax
import jax.numpy as jnp
import ml_dtypes
import numpy as np
from jax import lax
from jax.experimental import pallas as pl
from jax.experimental.pallas import tpu as pltpu
from jax.sharding import PartitionSpec as P

screen = 1600.0
MESH = pl.DeviceIdType.MESH


def tables(count):
    index = np.arange(count)
    angle = (index[:, None] * index[None, :] % count) * (2.0 * math.pi / count)
    cosine, sine = np.cos(angle), np.sin(angle)
    ahead = np.block([[cosine, sine], [-sine, cosine]])
    back = np.block([[cosine, -sine], [sine, cosine]])
    out = []
    for matrix in (ahead, back):
        high = matrix.astype(ml_dtypes.bfloat16)
        low = (matrix - high.astype(np.float64)).astype(ml_dtypes.bfloat16)
        out.append(np.concatenate([high, low, high], axis=1))
        out.append(np.concatenate([high, low, high], axis=0))
    return out


def split(values):
    high = values.astype(jnp.bfloat16)
    low = (values - high.astype(jnp.float32)).astype(jnp.bfloat16)
    return high, low


def left(table, values):
    high, low = split(values)
    stacked = jnp.concatenate([high, high, low], axis=0)
    return jnp.dot(table[...], stacked, preferred_element_type=jnp.float32)


def right(values, table):
    high, low = split(values)
    stacked = jnp.concatenate([high, high, low], axis=1)
    return jnp.dot(stacked, table[...], preferred_element_type=jnp.float32)


def swap(values, count):
    top = jnp.concatenate([values[:count, :count], values[count:, :count]], axis=1)
    bottom = jnp.concatenate([values[:count, count:], values[count:, count:]], axis=1)
    return jnp.concatenate([top, bottom], axis=0)


def solution(mesh):
    groups = mesh.shape["grid"]
    bands = mesh.shape["band"]
    bits = bands.bit_length() - 1
    offsets = sorted(range(1, groups), key=lambda s: (abs(s - groups // 2), s))

    def kernel(
        targets, occupied, owners, mask, ahead_l, ahead_r, back_l, back_r,
        out,
        masked, arrived, orbital, spectra, lines, filtered, planes, coulomb,
        core_send, core_recv, wide_send, wide_recv, full_send, full_recv,
        go_send, go_recv, come_send, come_recv, own_sem,
    ):
        count = targets.shape[2]
        slab = targets.shape[1]
        half = slab // 2
        window = owners.shape[0]
        per_group = occupied.shape[0]
        band = lax.axis_index("band")
        grid = lax.axis_index("grid")

        def partner(bit):
            step = 1 << bit
            return band + step - 2 * step * lax.rem(lax.div(band, step), 2)

        barrier = pltpu.get_barrier_semaphore()
        for bit in range(bits):
            pl.semaphore_signal(barrier, inc=1, device_id=(partner(bit), grid), device_id_type=MESH)
        for s in offsets:
            pl.semaphore_signal(
                barrier, inc=1, device_id=(band, lax.rem(grid + s, groups)), device_id_type=MESH
            )

        mine = lax.rem(band, 2) * half
        other = half - mine

        def hide(w):
            @pl.loop(0, slab)
            def _(a):
                total = jnp.zeros((count, count), jnp.float32)
                for j in range(per_group):
                    total += jnp.where(owners[w] == band * per_group + j, occupied[j, a], 0.0)
                masked[w, a] = total

        def core_copy(w):
            return pltpu.make_async_remote_copy(
                src_ref=masked.at[w, pl.ds(other, half)],
                dst_ref=arrived.at[0, w],
                send_sem=core_send.at[w], recv_sem=core_recv.at[w],
                device_id=(partner(0), grid), device_id_type=MESH,
            )

        def wide_copy(w, bit):
            return pltpu.make_async_remote_copy(
                src_ref=orbital.at[w, pl.ds(mine, half)] if bit == 1 else masked.at[w, pl.ds(mine, half)],
                dst_ref=arrived.at[bit, w],
                send_sem=wide_send.at[w, bit], recv_sem=wide_recv.at[w, bit],
                device_id=(partner(bit), grid), device_id_type=MESH,
            )

        def full_copy(w):
            return pltpu.make_async_remote_copy(
                src_ref=orbital.at[w, pl.ds(mine, half)],
                dst_ref=orbital.at[w, pl.ds(mine, half)],
                send_sem=full_send.at[w], recv_sem=full_recv.at[w],
                device_id=(partner(0), grid), device_id_type=MESH,
            )

        def merge(w, bit, source, target):
            @pl.loop(0, half)
            def _(a):
                target[w, mine + a] = source[w, mine + a] + arrived[bit, w, a]

        hide(0)
        pl.semaphore_wait(barrier, bits + groups - 1)
        core_copy(0).start()
        for w in range(1, window):
            hide(w)

        def begin(w):
            if w > 0:
                core_copy(w).start()
            core_copy(w).wait()
            merge(w, 0, masked, orbital)
            wide_copy(w, 1).start()

        def settle(w):
            wide_copy(w, 1).wait()
            merge(w, 1, orbital, orbital)
            for bit in range(2, bits):
                @pl.loop(0, half)
                def _(a):
                    masked[w, mine + a] = orbital[w, mine + a]
                wide_copy(w, bit).start()
                wide_copy(w, bit).wait()
                merge(w, bit, orbital, orbital)
            full_copy(w).start()

        def forward(w):
            @pl.loop(0, slab // 2)
            def _(step):
                rows = []
                for p in range(2):
                    a = step * 2 + p
                    cells = orbital[w, a]
                    rows.append(jnp.concatenate([cells * targets[0, a], cells * targets[1, a]], axis=1))
                values = right(jnp.concatenate(rows, axis=0), back_r)
                values = left(ahead_l, swap(values, count))
                for p in range(2):
                    a = step * 2 + p
                    for part in range(2):
                        spectra[w, part, a] = values[part * count:(part + 1) * count, p * count:(p + 1) * count]

        def piece(source, landing, w, s, sends, recvs):
            peer = lax.rem(grid + s, groups)
            return pltpu.make_async_remote_copy(
                src_ref=source.at[w, :, :, pl.ds(pl.multiple_of(peer * slab, slab), slab), :],
                dst_ref=landing.at[w, :, pl.ds(grid * slab, slab), :, :],
                send_sem=sends.at[w, s], recv_sem=recvs.at[w, s],
                device_id=(band, peer), device_id_type=MESH,
            )

        def own(source, landing, w, k):
            return pltpu.make_async_copy(
                source.at[w, :, :, pl.ds(pl.multiple_of(grid * slab, slab), slab), :],
                landing.at[w, :, pl.ds(grid * slab, slab), :, :],
                own_sem.at[w, k],
            )

        def send(source, landing, w, k, sends, recvs):
            for s in offsets:
                piece(source, landing, w, s, sends, recvs).start()
            own(source, landing, w, k).start()

        def receive(source, landing, w, k, sends, recvs):
            own(source, landing, w, k).wait()
            for s in offsets:
                piece(source, landing, w, s, sends, recvs).wait_recv()

        def drain(source, landing, w, sends, recvs):
            for s in offsets:
                piece(source, landing, w, s, sends, recvs).wait_send()

        def load(flat, w, line):
            parts = []
            for part in range(2):
                parts.append(jnp.concatenate(
                    [flat[w, part, pl.ds(line + p, count, stride=slab), :] for p in range(2)], axis=1
                ))
            return jnp.concatenate(parts, axis=0)

        def build():
            flat = mask.reshape(count * slab, count)

            def signed(index):
                return jnp.where(index < count // 2, index, index - count)

            first = signed(lax.broadcasted_iota(jnp.int32, (count, count), 0))
            third = signed(lax.broadcasted_iota(jnp.int32, (count, count), 1))
            base = first * first + third * third
            scale = -1.0 / float(count * count * count)

            @pl.loop(0, slab)
            def _(b):
                second = signed(grid * slab + b)
                squared = (base + second * second).astype(jnp.float32)
                kept = flat[pl.ds(b, count, stride=slab), :].astype(jnp.float32)
                coulomb[b] = screen / (screen + squared) * kept * scale

        def middle(w):
            flat = lines.reshape(window, 2, count * slab, count)

            @pl.loop(0, slab // 2)
            def _(step):
                values = left(ahead_l, load(flat, w, step * 2))
                factor = jnp.concatenate([coulomb[step * 2], coulomb[step * 2 + 1]], axis=1)
                values = values * jnp.concatenate([factor, factor], axis=0)
                values = left(back_l, values)
                for p in range(2):
                    for part in range(2):
                        filtered[w, part, step * 2 + p] = values[
                            part * count:(part + 1) * count, p * count:(p + 1) * count
                        ]

        def backward(w):
            flat = planes.reshape(window, 2, count * slab, count)

            @pl.loop(0, slab // 2)
            def _(step):
                values = left(back_l, load(flat, w, step * 2))
                values = right(swap(values, count), ahead_r)
                for p in range(2):
                    a = step * 2 + p
                    cells = orbital[w, a]
                    for t in range(2):
                        term = cells * values[p * count:(p + 1) * count, t * count:(t + 1) * count]
                        if w == 0:
                            out[t, a] = term
                        else:
                            out[t, a] += term

        begin(0)
        settle(0)
        if window > 1:
            begin(1)
        for w in range(window):
            full_copy(w).wait()
            forward(w)
            send(spectra, lines, w, 0, go_send, go_recv)
            if w + 1 < window:
                settle(w + 1)
                if w + 2 < window:
                    begin(w + 2)
        build()
        for w in range(window):
            receive(spectra, lines, w, 0, go_send, go_recv)
            middle(w)
            send(filtered, planes, w, 1, come_send, come_recv)
        for w in range(window):
            receive(filtered, planes, w, 1, come_send, come_recv)
            backward(w)
        for w in range(window):
            drain(spectra, lines, w, go_send, go_recv)
            drain(filtered, planes, w, come_send, come_recv)

    def shards(targets, occupied, owners, cutoff_mask):
        count = targets.shape[2]
        slab = targets.shape[1]
        window = owners.shape[0]
        dma = pltpu.SemaphoreType.DMA
        vmem = pl.BlockSpec(memory_space=pltpu.VMEM)
        f32 = jnp.float32
        return pl.pallas_call(
            kernel,
            out_shape=jax.ShapeDtypeStruct(targets.shape, f32),
            in_specs=[vmem, vmem, pl.BlockSpec(memory_space=pltpu.SMEM)] + [vmem] * 5,
            out_specs=vmem,
            scratch_shapes=[
                pltpu.VMEM((window, slab, count, count), f32),
                pltpu.VMEM((bits, window, slab // 2, count, count), f32),
                pltpu.VMEM((window, slab, count, count), f32),
                pltpu.VMEM((window, 2, slab, count, count), f32),
                pltpu.VMEM((window, 2, count, slab, count), f32),
                pltpu.VMEM((window, 2, slab, count, count), f32),
                pltpu.VMEM((window, 2, count, slab, count), f32),
                pltpu.VMEM((slab, count, count), f32),
                dma((window,)), dma((window,)),
                dma((window, bits)), dma((window, bits)),
                dma((window,)), dma((window,)),
                dma((window, groups)), dma((window, groups)),
                dma((window, groups)), dma((window, groups)),
                dma((window, 2)),
            ],
            compiler_params=pltpu.CompilerParams(
                collective_id=0, has_side_effects=True, vmem_limit_bytes=56 * 1024 * 1024
            ),
            name="exchange",
        )(targets, occupied, owners, cutoff_mask, *[jnp.asarray(t) for t in tables(count)])

    return jax.shard_map(
        shards,
        mesh=mesh,
        in_specs=(
            P("band", "grid", None, None),
            P("band", "grid", None, None),
            P(),
            P(None, "grid", None),
        ),
        out_specs=P("band", "grid", None, None),
        check_vma=False,
    )
```

```python
import math

import jax
import jax.numpy as jnp
import ml_dtypes
import numpy as np
from jax import lax
from jax.experimental import pallas as pl
from jax.experimental.pallas import tpu as pltpu
from jax.sharding import PartitionSpec as P

screen = 1600.0
MESH = pl.DeviceIdType.MESH
quarters = 2


def tables(count):
    index = np.arange(count)
    angle = (index[:, None] * index[None, :] % count) * (2.0 * math.pi / count)
    cosine, sine = np.cos(angle), np.sin(angle)
    ahead = np.block([[cosine, sine], [-sine, cosine]])
    back = np.block([[cosine, -sine], [sine, cosine]])
    out = []
    for matrix in (ahead, back):
        high = matrix.astype(ml_dtypes.bfloat16)
        low = (matrix - high.astype(np.float64)).astype(ml_dtypes.bfloat16)
        out.append(np.concatenate([high, low, high], axis=1))
        out.append(np.concatenate([high, low, high], axis=0))
    return out


def split(values):
    high = values.astype(jnp.bfloat16)
    low = (values - high.astype(jnp.float32)).astype(jnp.bfloat16)
    return high, low


def left(table, values):
    high, low = split(values)
    stacked = jnp.concatenate([high, high, low], axis=0)
    return jnp.dot(table[...], stacked, preferred_element_type=jnp.float32)


def right(values, table):
    high, low = split(values)
    stacked = jnp.concatenate([high, high, low], axis=1)
    return jnp.dot(stacked, table[...], preferred_element_type=jnp.float32)


def swap(values, count):
    top = jnp.concatenate([values[:count, :count], values[count:, :count]], axis=1)
    bottom = jnp.concatenate([values[:count, count:], values[count:, count:]], axis=1)
    return jnp.concatenate([top, bottom], axis=0)


def solution(mesh):
    groups = mesh.shape["grid"]
    bands = mesh.shape["band"]
    bits = bands.bit_length() - 1
    offsets = sorted(range(1, groups), key=lambda s: (abs(s - groups // 2), s))

    def kernel(
        targets, occupied, owners, mask, ahead_l, ahead_r, back_l, back_r,
        out,
        masked, arrived, orbital, spectra, lines, filtered, planes, coulomb,
        core_send, core_recv, wide_send, wide_recv, full_send, full_recv,
        go_send, go_recv, come_send, come_recv, own_sem,
    ):
        count = targets.shape[2]
        slab = targets.shape[1]
        half = slab // 2
        sub = half // quarters
        window = owners.shape[0]
        per_group = occupied.shape[0]
        band = lax.axis_index("band")
        grid = lax.axis_index("grid")

        def partner(bit):
            step = 1 << bit
            return band + step - 2 * step * lax.rem(lax.div(band, step), 2)

        barrier = pltpu.get_barrier_semaphore()
        for bit in range(bits):
            pl.semaphore_signal(barrier, inc=1, device_id=(partner(bit), grid), device_id_type=MESH)
        for s in offsets:
            pl.semaphore_signal(
                barrier, inc=1, device_id=(band, lax.rem(grid + s, groups)), device_id_type=MESH
            )

        mine = lax.rem(band, 2) * half
        other = half - mine

        def hide(w, base):
            @pl.loop(base, base + half)
            def _(a):
                total = jnp.zeros((count, count), jnp.float32)
                for j in range(per_group):
                    total += jnp.where(owners[w] == band * per_group + j, occupied[j, a], 0.0)
                masked[w, a] = total

        def core_copy(w, q):
            return pltpu.make_async_remote_copy(
                src_ref=masked.at[w, pl.ds(other + q * sub, sub)],
                dst_ref=arrived.at[0, w, pl.ds(q * sub, sub)],
                send_sem=core_send.at[w, q], recv_sem=core_recv.at[w, q],
                device_id=(partner(0), grid), device_id_type=MESH,
            )

        def wide_copy(w, bit, q):
            return pltpu.make_async_remote_copy(
                src_ref=(orbital if bit == 1 else masked).at[w, pl.ds(mine + q * sub, sub)],
                dst_ref=arrived.at[bit, w, pl.ds(q * sub, sub)],
                send_sem=wide_send.at[w, bit, q], recv_sem=wide_recv.at[w, bit, q],
                device_id=(partner(bit), grid), device_id_type=MESH,
            )

        def full_copy(w, q):
            return pltpu.make_async_remote_copy(
                src_ref=orbital.at[w, pl.ds(mine + q * sub, sub)],
                dst_ref=orbital.at[w, pl.ds(mine + q * sub, sub)],
                send_sem=full_send.at[w, q], recv_sem=full_recv.at[w, q],
                device_id=(partner(0), grid), device_id_type=MESH,
            )

        def merge(w, bit, source, target, q):
            @pl.loop(q * sub, q * sub + sub)
            def _(a):
                target[w, mine + a] = source[w, mine + a] + arrived[bit, w, a]

        def begin(w):
            for q in range(quarters):
                core_copy(w, q).wait()
                merge(w, 0, masked, orbital, q)
                wide_copy(w, 1, q).start()

        def settle(w, q):
            wide_copy(w, 1, q).wait()
            merge(w, 1, orbital, orbital, q)
            for bit in range(2, bits):
                @pl.loop(q * sub, q * sub + sub)
                def _(a):
                    masked[w, mine + a] = orbital[w, mine + a]
                wide_copy(w, bit, q).start()
                wide_copy(w, bit, q).wait()
                merge(w, bit, orbital, orbital, q)
            full_copy(w, q).start()

        def forward(w, base):
            @pl.loop(0, sub // 2)
            def _(step):
                rows = []
                for p in range(2):
                    a = base + step * 2 + p
                    cells = orbital[w, a]
                    rows.append(jnp.concatenate([cells * targets[0, a], cells * targets[1, a]], axis=1))
                values = right(jnp.concatenate(rows, axis=0), back_r)
                values = left(ahead_l, swap(values, count))
                for p in range(2):
                    a = base + step * 2 + p
                    for part in range(2):
                        spectra[w, part, a] = values[part * count:(part + 1) * count, p * count:(p + 1) * count]

        def go(w, s, k):
            peer = lax.rem(grid + s, groups)
            base = (other if k % 2 else mine) + (k // 2) * sub
            return pltpu.make_async_remote_copy(
                src_ref=spectra.at[w, :, pl.ds(base, sub), pl.ds(pl.multiple_of(peer * slab, slab), slab), :],
                dst_ref=lines.at[w, :, pl.ds(grid * slab + base, sub), :, :],
                send_sem=go_send.at[w, s, k], recv_sem=go_recv.at[w, s, k],
                device_id=(band, peer), device_id_type=MESH,
            )

        def come(w, s, h):
            peer = lax.rem(grid + s, groups)
            first, deep, row, high = 0, slab, 0, slab
            if w + 1 < window:
                first, deep = h * half, half
            elif cuts(w) > 1:
                row, high = h * half, half
            return pltpu.make_async_remote_copy(
                src_ref=filtered.at[
                    w, :, pl.ds(first, deep), pl.ds(pl.multiple_of(peer * slab + row, high), high), :
                ],
                dst_ref=planes.at[w, :, pl.ds(grid * slab + first, deep), pl.ds(row, high), :],
                send_sem=come_send.at[w, s, h], recv_sem=come_recv.at[w, s, h],
                device_id=(band, peer), device_id_type=MESH,
            )

        def cuts(w):
            return 2 if w + 1 < window or slab % 16 == 0 else 1

        def own(source, landing, w, k):
            return pltpu.make_async_copy(
                source.at[w, :, :, pl.ds(pl.multiple_of(grid * slab, slab), slab), :],
                landing.at[w, :, pl.ds(grid * slab, slab), :, :],
                own_sem.at[w, k],
            )

        def load(flat, w, line):
            parts = []
            for part in range(2):
                parts.append(jnp.concatenate(
                    [flat[w, part, pl.ds(line + p, count, stride=slab), :] for p in range(2)], axis=1
                ))
            return jnp.concatenate(parts, axis=0)

        def build():
            flat = mask.reshape(count * slab, count)

            def signed(index):
                return jnp.where(index < count // 2, index, index - count)

            first = signed(lax.broadcasted_iota(jnp.int32, (count, count), 0))
            third = signed(lax.broadcasted_iota(jnp.int32, (count, count), 1))
            base = first * first + third * third
            scale = -1.0 / float(count * count * count)

            @pl.loop(0, slab)
            def _(b):
                second = signed(grid * slab + b)
                squared = (base + second * second).astype(jnp.float32)
                kept = flat[pl.ds(b, count, stride=slab), :].astype(jnp.float32)
                coulomb[b] = screen / (screen + squared) * kept * scale

        def middle(w, base, extent):
            flat = lines.reshape(window, 2, count * slab, count)

            @pl.loop(base // 2, (base + extent) // 2)
            def _(step):
                values = left(ahead_l, load(flat, w, step * 2))
                factor = jnp.concatenate([coulomb[step * 2], coulomb[step * 2 + 1]], axis=1)
                values = values * jnp.concatenate([factor, factor], axis=0)
                values = left(back_l, values)
                for p in range(2):
                    for part in range(2):
                        filtered[w, part, step * 2 + p] = values[
                            part * count:(part + 1) * count, p * count:(p + 1) * count
                        ]

        def backward(w, base, extent):
            flat = planes.reshape(window, 2, count * slab, count)

            @pl.loop(base // 2, (base + extent) // 2)
            def _(step):
                values = left(back_l, load(flat, w, step * 2))
                values = right(swap(values, count), ahead_r)
                for p in range(2):
                    a = step * 2 + p
                    cells = orbital[w, a]
                    for t in range(2):
                        term = cells * values[p * count:(p + 1) * count, t * count:(t + 1) * count]
                        if w == 0:
                            out[t, a] = term
                        else:
                            out[t, a] += term

        hide(0, other)
        pl.semaphore_wait(barrier, bits + groups - 1)
        for q in range(quarters):
            core_copy(0, q).start()
        hide(0, mine)
        begin(0)
        for w in range(1, window):
            hide(w, other)
            for q in range(quarters):
                core_copy(w, q).start()
            hide(w, mine)
        for w in range(window):
            for q in range(quarters):
                settle(w, q)
                if q + 1 == quarters and w + 1 < window:
                    begin(w + 1)
                forward(w, mine + q * sub)
                for s in offsets:
                    go(w, s, 2 * q).start()
                full_copy(w, q).wait()
                forward(w, other + q * sub)
                for s in offsets:
                    go(w, s, 2 * q + 1).start()
            own(spectra, lines, w, 0).start()
        build()
        for w in range(window):
            own(spectra, lines, w, 0).wait()
            for k in range(2 * quarters):
                for s in offsets:
                    go(w, s, k).wait_recv()
            if w + 1 < window:
                for h in range(2):
                    middle(w, h * half, half)
                    for s in offsets:
                        come(w, s, h).start()
            else:
                middle(w, 0, slab)
                for h in range(cuts(w)):
                    for s in offsets:
                        come(w, s, h).start()
            own(filtered, planes, w, 1).start()
        for w in range(window):
            own(filtered, planes, w, 1).wait()
            if w + 1 < window or cuts(w) == 1:
                for h in range(cuts(w)):
                    for s in offsets:
                        come(w, s, h).wait_recv()
                backward(w, 0, slab)
            else:
                for h in range(2):
                    for s in offsets:
                        come(w, s, h).wait_recv()
                    backward(w, h * half, half)
        for w in range(window):
            for s in offsets:
                for k in range(2 * quarters):
                    go(w, s, k).wait_send()
                for h in range(cuts(w)):
                    come(w, s, h).wait_send()

    def shards(targets, occupied, owners, cutoff_mask):
        count = targets.shape[2]
        slab = targets.shape[1]
        window = owners.shape[0]
        dma = pltpu.SemaphoreType.DMA
        vmem = pl.BlockSpec(memory_space=pltpu.VMEM)
        f32 = jnp.float32
        return pl.pallas_call(
            kernel,
            out_shape=jax.ShapeDtypeStruct(targets.shape, f32),
            in_specs=[vmem, vmem, pl.BlockSpec(memory_space=pltpu.SMEM)] + [vmem] * 5,
            out_specs=vmem,
            scratch_shapes=[
                pltpu.VMEM((window, slab, count, count), f32),
                pltpu.VMEM((bits, window, slab // 2, count, count), f32),
                pltpu.VMEM((window, slab, count, count), f32),
                pltpu.VMEM((window, 2, slab, count, count), f32),
                pltpu.VMEM((window, 2, count, slab, count), f32),
                pltpu.VMEM((window, 2, slab, count, count), f32),
                pltpu.VMEM((window, 2, count, slab, count), f32),
                pltpu.VMEM((slab, count, count), f32),
                dma((window, quarters)), dma((window, quarters)),
                dma((window, bits, quarters)), dma((window, bits, quarters)),
                dma((window, quarters)), dma((window, quarters)),
                dma((window, groups, 2 * quarters)), dma((window, groups, 2 * quarters)),
                dma((window, groups, 2)), dma((window, groups, 2)),
                dma((window, 2)),
            ],
            compiler_params=pltpu.CompilerParams(
                collective_id=0, has_side_effects=True, vmem_limit_bytes=56 * 1024 * 1024
            ),
            name="exchange",
        )(targets, occupied, owners, cutoff_mask, *[jnp.asarray(t) for t in tables(count)])

    return jax.shard_map(
        shards,
        mesh=mesh,
        in_specs=(
            P("band", "grid", None, None),
            P("band", "grid", None, None),
            P(),
            P(None, "grid", None),
        ),
        out_specs=P("band", "grid", None, None),
        check_vma=False,
    )
```

```python
import math

import jax
import jax.numpy as jnp
import ml_dtypes
import numpy as np
from jax import lax
from jax.experimental import pallas as pl
from jax.experimental.pallas import tpu as pltpu
from jax.sharding import PartitionSpec as P

screen = 1600.0
MESH = pl.DeviceIdType.MESH
most = 4


def tables(count):
    index = np.arange(count)
    angle = (index[:, None] * index[None, :] % count) * (2.0 * math.pi / count)
    cosine, sine = np.cos(angle), np.sin(angle)
    ahead = np.block([[cosine, sine], [-sine, cosine]])
    back = np.block([[cosine, -sine], [sine, cosine]])
    out = []
    for matrix in (ahead, back):
        high = matrix.astype(ml_dtypes.bfloat16)
        low = (matrix - high.astype(np.float64)).astype(ml_dtypes.bfloat16)
        out.append(np.concatenate([high, low, high], axis=1))
        out.append(np.concatenate([high, low, high], axis=0))
    return out


def split(values):
    high = values.astype(jnp.bfloat16)
    low = (values - high.astype(jnp.float32)).astype(jnp.bfloat16)
    return high, low


def left(table, values):
    high, low = split(values)
    stacked = jnp.concatenate([high, high, low], axis=0)
    return jnp.dot(table[...], stacked, preferred_element_type=jnp.float32)


def right(values, table):
    high, low = split(values)
    stacked = jnp.concatenate([high, high, low], axis=1)
    return jnp.dot(stacked, table[...], preferred_element_type=jnp.float32)


def swap(values, count):
    top = jnp.concatenate([values[:count, :count], values[count:, :count]], axis=1)
    bottom = jnp.concatenate([values[:count, count:], values[count:, count:]], axis=1)
    return jnp.concatenate([top, bottom], axis=0)


def solution(mesh):
    groups = mesh.shape["grid"]
    bands = mesh.shape["band"]
    bits = bands.bit_length() - 1
    offsets = sorted(range(1, groups), key=lambda s: (abs(s - groups // 2), s))

    def kernel(
        targets_in, occupied, owners, mask_in, ahead_l_in, ahead_r_in, back_l_in, back_r_in,
        out,
        targets, mask, ahead_l, ahead_r, back_l, back_r,
        masked, arrived, orbital, spectra, lines, filtered, planes, coulomb,
        core_send, core_recv, wide_send, wide_recv, full_send, full_recv,
        go_send, go_recv, come_send, come_recv, own_sem, load_sem,
    ):
        staged = [
            pltpu.make_async_copy(source, landing, load_sem.at[k])
            for k, (source, landing) in enumerate((
                (targets_in, targets), (back_r_in, back_r), (ahead_l_in, ahead_l),
                (mask_in, mask), (back_l_in, back_l), (ahead_r_in, ahead_r),
            ))
        ]
        for copy in staged:
            copy.start()
        count = targets.shape[2]
        slab = targets.shape[1]
        half = slab // 2

        def pieces(w):
            return min(most if w == 0 else 2, half // 2)

        window = owners.shape[0]
        per_group = occupied.shape[0]
        band = lax.axis_index("band")
        grid = lax.axis_index("grid")

        def partner(bit):
            step = 1 << bit
            return band + step - 2 * step * lax.rem(lax.div(band, step), 2)

        barrier = pltpu.get_barrier_semaphore()
        for bit in range(bits):
            pl.semaphore_signal(barrier, inc=1, device_id=(partner(bit), grid), device_id_type=MESH)
        for s in offsets:
            pl.semaphore_signal(
                barrier, inc=1, device_id=(band, lax.rem(grid + s, groups)), device_id_type=MESH
            )

        mine = lax.rem(band, 2) * half
        other = half - mine

        def hide(w, base):
            @pl.loop(base, base + half)
            def _(a):
                total = jnp.zeros((count, count), jnp.float32)
                for j in range(per_group):
                    total += jnp.where(owners[w] == band * per_group + j, occupied[j, a], 0.0)
                masked[w, a] = total

        def core_copy(w, q):
            sub = half // pieces(w)
            return pltpu.make_async_remote_copy(
                src_ref=masked.at[w, pl.ds(other + q * sub, sub)],
                dst_ref=arrived.at[0, w, pl.ds(q * sub, sub)],
                send_sem=core_send.at[w, q], recv_sem=core_recv.at[w, q],
                device_id=(partner(0), grid), device_id_type=MESH,
            )

        def wide_copy(w, bit, q):
            sub = half // pieces(w)
            return pltpu.make_async_remote_copy(
                src_ref=(orbital if bit == 1 else masked).at[w, pl.ds(mine + q * sub, sub)],
                dst_ref=arrived.at[bit, w, pl.ds(q * sub, sub)],
                send_sem=wide_send.at[w, bit, q], recv_sem=wide_recv.at[w, bit, q],
                device_id=(partner(bit), grid), device_id_type=MESH,
            )

        def full_copy(w, q):
            sub = half // pieces(w)
            return pltpu.make_async_remote_copy(
                src_ref=orbital.at[w, pl.ds(mine + q * sub, sub)],
                dst_ref=orbital.at[w, pl.ds(mine + q * sub, sub)],
                send_sem=full_send.at[w, q], recv_sem=full_recv.at[w, q],
                device_id=(partner(0), grid), device_id_type=MESH,
            )

        def merge(w, bit, source, target, q):
            sub = half // pieces(w)
            @pl.loop(q * sub, q * sub + sub)
            def _(a):
                target[w, mine + a] = source[w, mine + a] + arrived[bit, w, a]

        def begin(w):
            for q in range(pieces(w)):
                core_copy(w, q).wait()
                merge(w, 0, masked, orbital, q)
                wide_copy(w, 1, q).start()

        def settle(w, q):
            sub = half // pieces(w)
            wide_copy(w, 1, q).wait()
            merge(w, 1, orbital, orbital, q)
            for bit in range(2, bits):
                @pl.loop(q * sub, q * sub + sub)
                def _(a):
                    masked[w, mine + a] = orbital[w, mine + a]
                wide_copy(w, bit, q).start()
                wide_copy(w, bit, q).wait()
                merge(w, bit, orbital, orbital, q)
            full_copy(w, q).start()

        def forward(w, base):
            sub = half // pieces(w)
            @pl.loop(0, sub // 2)
            def _(step):
                rows = []
                for p in range(2):
                    a = base + step * 2 + p
                    cells = orbital[w, a]
                    rows.append(jnp.concatenate([cells * targets[0, a], cells * targets[1, a]], axis=1))
                values = right(jnp.concatenate(rows, axis=0), back_r)
                values = left(ahead_l, swap(values, count))
                for p in range(2):
                    a = base + step * 2 + p
                    for part in range(2):
                        spectra[w, part, a] = values[part * count:(part + 1) * count, p * count:(p + 1) * count]

        def go(w, s, k):
            sub = half // pieces(w)
            peer = lax.rem(grid + s, groups)
            base = (other if k % 2 else mine) + (k // 2) * sub
            return pltpu.make_async_remote_copy(
                src_ref=spectra.at[w, :, pl.ds(base, sub), pl.ds(pl.multiple_of(peer * slab, slab), slab), :],
                dst_ref=lines.at[w, :, pl.ds(grid * slab + base, sub), :, :],
                send_sem=go_send.at[w, s, k], recv_sem=go_recv.at[w, s, k],
                device_id=(band, peer), device_id_type=MESH,
            )

        def come(w, s, h):
            peer = lax.rem(grid + s, groups)
            first, deep, row, high = 0, slab, 0, slab
            if w + 1 < window:
                first, deep = h * half, half
            elif cuts(w) > 1:
                row, high = h * half, half
            return pltpu.make_async_remote_copy(
                src_ref=filtered.at[
                    w, :, pl.ds(first, deep), pl.ds(pl.multiple_of(peer * slab + row, high), high), :
                ],
                dst_ref=planes.at[w, :, pl.ds(grid * slab + first, deep), pl.ds(row, high), :],
                send_sem=come_send.at[w, s, h], recv_sem=come_recv.at[w, s, h],
                device_id=(band, peer), device_id_type=MESH,
            )

        def cuts(w):
            return 2 if w + 1 < window or slab % 16 == 0 else 1

        def own(source, landing, w, k):
            return pltpu.make_async_copy(
                source.at[w, :, :, pl.ds(pl.multiple_of(grid * slab, slab), slab), :],
                landing.at[w, :, pl.ds(grid * slab, slab), :, :],
                own_sem.at[w, k],
            )

        def load(flat, w, line):
            parts = []
            for part in range(2):
                parts.append(jnp.concatenate(
                    [flat[w, part, pl.ds(line + p, count, stride=slab), :] for p in range(2)], axis=1
                ))
            return jnp.concatenate(parts, axis=0)

        def build():
            flat = mask.reshape(count * slab, count)

            def signed(index):
                return jnp.where(index < count // 2, index, index - count)

            first = signed(lax.broadcasted_iota(jnp.int32, (count, count), 0))
            third = signed(lax.broadcasted_iota(jnp.int32, (count, count), 1))
            base = first * first + third * third
            scale = -1.0 / float(count * count * count)

            @pl.loop(0, slab)
            def _(b):
                second = signed(grid * slab + b)
                squared = (base + second * second).astype(jnp.float32)
                kept = flat[pl.ds(b, count, stride=slab), :].astype(jnp.float32)
                coulomb[b] = screen / (screen + squared) * kept * scale

        def middle(w, base, extent):
            flat = lines.reshape(window, 2, count * slab, count)

            @pl.loop(base // 2, (base + extent) // 2)
            def _(step):
                values = left(ahead_l, load(flat, w, step * 2))
                factor = jnp.concatenate([coulomb[step * 2], coulomb[step * 2 + 1]], axis=1)
                values = values * jnp.concatenate([factor, factor], axis=0)
                values = left(back_l, values)
                for p in range(2):
                    for part in range(2):
                        filtered[w, part, step * 2 + p] = values[
                            part * count:(part + 1) * count, p * count:(p + 1) * count
                        ]

        def backward(w, base, extent):
            flat = planes.reshape(window, 2, count * slab, count)

            @pl.loop(base // 2, (base + extent) // 2)
            def _(step):
                values = left(back_l, load(flat, w, step * 2))
                values = right(swap(values, count), ahead_r)
                for p in range(2):
                    a = step * 2 + p
                    cells = orbital[w, a]
                    for t in range(2):
                        term = cells * values[p * count:(p + 1) * count, t * count:(t + 1) * count]
                        if w == 0:
                            out[t, a] = term
                        else:
                            out[t, a] += term

        hide(0, other)
        pl.semaphore_wait(barrier, bits + groups - 1)
        for q in range(pieces(0)):
            core_copy(0, q).start()
        hide(0, mine)
        begin(0)
        for w in range(1, window):
            hide(w, other)
            for q in range(pieces(w)):
                core_copy(w, q).start()
            hide(w, mine)
        for copy in staged[:3]:
            copy.wait()
        for w in range(window):
            sub = half // pieces(w)
            for q in range(pieces(w)):
                settle(w, q)
                if q + 1 == pieces(w) and w + 1 < window:
                    begin(w + 1)
                forward(w, mine + q * sub)
                for s in offsets:
                    go(w, s, 2 * q).start()
                full_copy(w, q).wait()
                forward(w, other + q * sub)
                for s in offsets:
                    go(w, s, 2 * q + 1).start()
            own(spectra, lines, w, 0).start()
        for copy in staged[3:]:
            copy.wait()
        build()
        for w in range(window):
            own(spectra, lines, w, 0).wait()
            for k in range(2 * pieces(w)):
                for s in offsets:
                    go(w, s, k).wait_recv()
            if w + 1 < window:
                for h in range(2):
                    middle(w, h * half, half)
                    for s in offsets:
                        come(w, s, h).start()
            else:
                middle(w, 0, slab)
                for h in range(cuts(w)):
                    for s in offsets:
                        come(w, s, h).start()
            own(filtered, planes, w, 1).start()
        for w in range(window):
            own(filtered, planes, w, 1).wait()
            if w + 1 < window or cuts(w) == 1:
                for h in range(cuts(w)):
                    for s in offsets:
                        come(w, s, h).wait_recv()
                backward(w, 0, slab)
            else:
                for h in range(2):
                    for s in offsets:
                        come(w, s, h).wait_recv()
                    backward(w, h * half, half)
        for w in range(window):
            for s in offsets:
                for k in range(2 * pieces(w)):
                    go(w, s, k).wait_send()
                for h in range(cuts(w)):
                    come(w, s, h).wait_send()

    def shards(targets, occupied, owners, cutoff_mask):
        count = targets.shape[2]
        slab = targets.shape[1]
        window = owners.shape[0]
        dma = pltpu.SemaphoreType.DMA
        vmem = pl.BlockSpec(memory_space=pltpu.VMEM)
        far = pl.BlockSpec(memory_space=pl.ANY)
        f32 = jnp.float32
        wide, tall = (2 * count, 6 * count), (6 * count, 2 * count)
        return pl.pallas_call(
            kernel,
            out_shape=jax.ShapeDtypeStruct(targets.shape, f32),
            in_specs=[far, vmem, pl.BlockSpec(memory_space=pltpu.SMEM)] + [far] * 5,
            out_specs=vmem,
            scratch_shapes=[
                pltpu.VMEM(targets.shape, f32),
                pltpu.VMEM(cutoff_mask.shape, jnp.int32),
                pltpu.VMEM(wide, jnp.bfloat16), pltpu.VMEM(tall, jnp.bfloat16),
                pltpu.VMEM(wide, jnp.bfloat16), pltpu.VMEM(tall, jnp.bfloat16),
                pltpu.VMEM((window, slab, count, count), f32),
                pltpu.VMEM((bits, window, slab // 2, count, count), f32),
                pltpu.VMEM((window, slab, count, count), f32),
                pltpu.VMEM((window, 2, slab, count, count), f32),
                pltpu.VMEM((window, 2, count, slab, count), f32),
                pltpu.VMEM((window, 2, slab, count, count), f32),
                pltpu.VMEM((window, 2, count, slab, count), f32),
                pltpu.VMEM((slab, count, count), f32),
                dma((window, most)), dma((window, most)),
                dma((window, bits, most)), dma((window, bits, most)),
                dma((window, most)), dma((window, most)),
                dma((window, groups, 2 * most)), dma((window, groups, 2 * most)),
                dma((window, groups, 2)), dma((window, groups, 2)),
                dma((window, 2)), dma((6,)),
            ],
            compiler_params=pltpu.CompilerParams(
                collective_id=0, has_side_effects=True, vmem_limit_bytes=56 * 1024 * 1024
            ),
            name="exchange",
        )(targets, occupied, owners, cutoff_mask, *[jnp.asarray(t) for t in tables(count)])

    return jax.shard_map(
        shards,
        mesh=mesh,
        in_specs=(
            P("band", "grid", None, None),
            P("band", "grid", None, None),
            P(),
            P(None, "grid", None),
        ),
        out_specs=P("band", "grid", None, None),
        check_vma=False,
    )
```

```python
import math

import jax
import jax.numpy as jnp
import ml_dtypes
import numpy as np
from jax import lax
from jax.experimental import pallas as pl
from jax.experimental.pallas import tpu as pltpu
from jax.sharding import PartitionSpec as P

screen = 1600.0
MESH = pl.DeviceIdType.MESH
most = 4


def tables(count):
    index = np.arange(count)
    angle = (index[:, None] * index[None, :] % count) * (2.0 * math.pi / count)
    cosine, sine = np.cos(angle), np.sin(angle)
    ahead = np.block([[cosine, sine], [-sine, cosine]])
    back = np.block([[cosine, -sine], [sine, cosine]])
    out = []
    for matrix in (ahead, back):
        high = matrix.astype(ml_dtypes.bfloat16)
        low = (matrix - high.astype(np.float64)).astype(ml_dtypes.bfloat16)
        out.append(np.concatenate([high, low, high], axis=1))
        out.append(np.concatenate([high, low, high], axis=0))
    return out


def split(values):
    high = values.astype(jnp.bfloat16)
    low = (values - high.astype(jnp.float32)).astype(jnp.bfloat16)
    return high, low


def left(table, values):
    high, low = split(values)
    stacked = jnp.concatenate([high, high, low], axis=0)
    return jnp.dot(table[...], stacked, preferred_element_type=jnp.float32)


def right(values, table):
    high, low = split(values)
    stacked = jnp.concatenate([high, high, low], axis=1)
    return jnp.dot(stacked, table[...], preferred_element_type=jnp.float32)


def swap(values, count):
    top = jnp.concatenate([values[:count, :count], values[count:, :count]], axis=1)
    bottom = jnp.concatenate([values[:count, count:], values[count:, count:]], axis=1)
    return jnp.concatenate([top, bottom], axis=0)


def solution(mesh):
    groups = mesh.shape["grid"]
    bands = mesh.shape["band"]
    bits = bands.bit_length() - 1
    offsets = sorted(range(1, groups), key=lambda s: (abs(s - groups // 2), s))

    def kernel(
        targets_in, occupied, owners, mask_in, ahead_l_in, ahead_r_in, back_l_in, back_r_in,
        out_far,
        out, targets, mask, ahead_l, ahead_r, back_l, back_r,
        masked, arrived, orbital, spectra, lines, filtered, planes, coulomb,
        core_send, core_recv, wide_send, wide_recv, full_send, full_recv,
        go_send, go_recv, come_send, come_recv, own_sem, load_sem, store_sem,
    ):
        staged = [
            pltpu.make_async_copy(source, landing, load_sem.at[k])
            for k, (source, landing) in enumerate((
                (targets_in, targets), (back_r_in, back_r), (ahead_l_in, ahead_l),
                (mask_in, mask), (back_l_in, back_l), (ahead_r_in, ahead_r),
            ))
        ]
        for copy in staged:
            copy.start()
        count = targets.shape[2]
        slab = targets.shape[1]
        half = slab // 2

        def pieces(w):
            return min(most if w == 0 else 2, half // 2)

        window = owners.shape[0]
        per_group = occupied.shape[0]
        band = lax.axis_index("band")
        grid = lax.axis_index("grid")

        def partner(bit):
            step = 1 << bit
            return band + step - 2 * step * lax.rem(lax.div(band, step), 2)

        barrier = pltpu.get_barrier_semaphore()
        for bit in range(bits):
            pl.semaphore_signal(barrier, inc=1, device_id=(partner(bit), grid), device_id_type=MESH)
        for s in offsets:
            pl.semaphore_signal(
                barrier, inc=1, device_id=(band, lax.rem(grid + s, groups)), device_id_type=MESH
            )

        mine = lax.rem(band, 2) * half
        other = half - mine

        def hide(w, base):
            @pl.loop(base, base + half)
            def _(a):
                total = jnp.zeros((count, count), jnp.float32)
                for j in range(per_group):
                    total += jnp.where(owners[w] == band * per_group + j, occupied[j, a], 0.0)
                masked[w, a] = total

        def core_copy(w, q):
            sub = half // pieces(w)
            return pltpu.make_async_remote_copy(
                src_ref=masked.at[w, pl.ds(other + q * sub, sub)],
                dst_ref=arrived.at[0, w, pl.ds(q * sub, sub)],
                send_sem=core_send.at[w, q], recv_sem=core_recv.at[w, q],
                device_id=(partner(0), grid), device_id_type=MESH,
            )

        def wide_copy(w, bit, q):
            sub = half // pieces(w)
            return pltpu.make_async_remote_copy(
                src_ref=(orbital if bit == 1 else masked).at[w, pl.ds(mine + q * sub, sub)],
                dst_ref=arrived.at[bit, w, pl.ds(q * sub, sub)],
                send_sem=wide_send.at[w, bit, q], recv_sem=wide_recv.at[w, bit, q],
                device_id=(partner(bit), grid), device_id_type=MESH,
            )

        def full_copy(w, q):
            sub = half // pieces(w)
            return pltpu.make_async_remote_copy(
                src_ref=orbital.at[w, pl.ds(mine + q * sub, sub)],
                dst_ref=orbital.at[w, pl.ds(mine + q * sub, sub)],
                send_sem=full_send.at[w, q], recv_sem=full_recv.at[w, q],
                device_id=(partner(0), grid), device_id_type=MESH,
            )

        def merge(w, bit, source, target, q):
            sub = half // pieces(w)
            @pl.loop(q * sub, q * sub + sub)
            def _(a):
                target[w, mine + a] = source[w, mine + a] + arrived[bit, w, a]

        def begin(w):
            for q in range(pieces(w)):
                core_copy(w, q).wait()
                merge(w, 0, masked, orbital, q)
                wide_copy(w, 1, q).start()

        def settle(w, q):
            sub = half // pieces(w)
            wide_copy(w, 1, q).wait()
            merge(w, 1, orbital, orbital, q)
            for bit in range(2, bits):
                @pl.loop(q * sub, q * sub + sub)
                def _(a):
                    masked[w, mine + a] = orbital[w, mine + a]
                wide_copy(w, bit, q).start()
                wide_copy(w, bit, q).wait()
                merge(w, bit, orbital, orbital, q)
            full_copy(w, q).start()

        def forward(w, base):
            sub = half // pieces(w)
            @pl.loop(0, sub // 2)
            def _(step):
                rows = []
                for p in range(2):
                    a = base + step * 2 + p
                    cells = orbital[w, a]
                    rows.append(jnp.concatenate([cells * targets[0, a], cells * targets[1, a]], axis=1))
                values = right(jnp.concatenate(rows, axis=0), back_r)
                values = left(ahead_l, swap(values, count))
                for p in range(2):
                    a = base + step * 2 + p
                    for part in range(2):
                        spectra[w, part, a] = values[part * count:(part + 1) * count, p * count:(p + 1) * count]

        def go(w, s, k):
            sub = half // pieces(w)
            peer = lax.rem(grid + s, groups)
            base = (other if k % 2 else mine) + (k // 2) * sub
            return pltpu.make_async_remote_copy(
                src_ref=spectra.at[w, :, pl.ds(base, sub), pl.ds(pl.multiple_of(peer * slab, slab), slab), :],
                dst_ref=lines.at[w, :, pl.ds(grid * slab + base, sub), :, :],
                send_sem=go_send.at[w, s, k], recv_sem=go_recv.at[w, s, k],
                device_id=(band, peer), device_id_type=MESH,
            )

        def come(w, s, h):
            peer = lax.rem(grid + s, groups)
            first, deep, row, high = 0, slab, 0, slab
            if w + 1 < window:
                first, deep = h * half, half
            elif cuts(w) > 1:
                row, high = h * half, half
            return pltpu.make_async_remote_copy(
                src_ref=filtered.at[
                    w, :, pl.ds(first, deep), pl.ds(pl.multiple_of(peer * slab + row, high), high), :
                ],
                dst_ref=planes.at[w, :, pl.ds(grid * slab + first, deep), pl.ds(row, high), :],
                send_sem=come_send.at[w, s, h], recv_sem=come_recv.at[w, s, h],
                device_id=(band, peer), device_id_type=MESH,
            )

        def cuts(w):
            return 2 if w + 1 < window or slab % 16 == 0 else 1

        def store(h):
            return pltpu.make_async_copy(
                out.at[:, pl.ds(h * half, half)], out_far.at[:, pl.ds(h * half, half)], store_sem.at[h]
            )

        def own(source, landing, w, k):
            return pltpu.make_async_copy(
                source.at[w, :, :, pl.ds(pl.multiple_of(grid * slab, slab), slab), :],
                landing.at[w, :, pl.ds(grid * slab, slab), :, :],
                own_sem.at[w, k],
            )

        def load(flat, w, line):
            parts = []
            for part in range(2):
                parts.append(jnp.concatenate(
                    [flat[w, part, pl.ds(line + p, count, stride=slab), :] for p in range(2)], axis=1
                ))
            return jnp.concatenate(parts, axis=0)

        def build():
            flat = mask.reshape(count * slab, count)

            def signed(index):
                return jnp.where(index < count // 2, index, index - count)

            first = signed(lax.broadcasted_iota(jnp.int32, (count, count), 0))
            third = signed(lax.broadcasted_iota(jnp.int32, (count, count), 1))
            base = first * first + third * third
            scale = -1.0 / float(count * count * count)

            @pl.loop(0, slab)
            def _(b):
                second = signed(grid * slab + b)
                squared = (base + second * second).astype(jnp.float32)
                kept = flat[pl.ds(b, count, stride=slab), :].astype(jnp.float32)
                coulomb[b] = screen / (screen + squared) * kept * scale

        def middle(w, base, extent):
            flat = lines.reshape(window, 2, count * slab, count)

            @pl.loop(base // 2, (base + extent) // 2)
            def _(step):
                values = left(ahead_l, load(flat, w, step * 2))
                factor = jnp.concatenate([coulomb[step * 2], coulomb[step * 2 + 1]], axis=1)
                values = values * jnp.concatenate([factor, factor], axis=0)
                values = left(back_l, values)
                for p in range(2):
                    for part in range(2):
                        filtered[w, part, step * 2 + p] = values[
                            part * count:(part + 1) * count, p * count:(p + 1) * count
                        ]

        def backward(w, base, extent):
            flat = planes.reshape(window, 2, count * slab, count)

            @pl.loop(base // 2, (base + extent) // 2)
            def _(step):
                values = left(back_l, load(flat, w, step * 2))
                values = right(swap(values, count), ahead_r)
                for p in range(2):
                    a = step * 2 + p
                    cells = orbital[w, a]
                    for t in range(2):
                        term = cells * values[p * count:(p + 1) * count, t * count:(t + 1) * count]
                        if w == 0:
                            out[t, a] = term
                        else:
                            out[t, a] += term

        hide(0, other)
        pl.semaphore_wait(barrier, bits + groups - 1)
        for q in range(pieces(0)):
            core_copy(0, q).start()
        hide(0, mine)
        begin(0)
        for w in range(1, window):
            hide(w, other)
            for q in range(pieces(w)):
                core_copy(w, q).start()
            hide(w, mine)
        for copy in staged[:3]:
            copy.wait()
        for w in range(window):
            sub = half // pieces(w)
            for q in range(pieces(w)):
                settle(w, q)
                if q + 1 == pieces(w) and w + 1 < window:
                    begin(w + 1)
                forward(w, mine + q * sub)
                for s in offsets:
                    go(w, s, 2 * q).start()
                full_copy(w, q).wait()
                forward(w, other + q * sub)
                for s in offsets:
                    go(w, s, 2 * q + 1).start()
            own(spectra, lines, w, 0).start()
        for copy in staged[3:]:
            copy.wait()
        build()
        for w in range(window):
            own(spectra, lines, w, 0).wait()
            for k in range(2 * pieces(w)):
                for s in offsets:
                    go(w, s, k).wait_recv()
            if w + 1 < window:
                for h in range(2):
                    middle(w, h * half, half)
                    for s in offsets:
                        come(w, s, h).start()
            else:
                middle(w, 0, slab)
                for h in range(cuts(w)):
                    for s in offsets:
                        come(w, s, h).start()
            own(filtered, planes, w, 1).start()
        for w in range(window):
            own(filtered, planes, w, 1).wait()
            if w + 1 < window or cuts(w) == 1:
                for h in range(cuts(w)):
                    for s in offsets:
                        come(w, s, h).wait_recv()
                backward(w, 0, slab)
            else:
                for h in range(2):
                    for s in offsets:
                        come(w, s, h).wait_recv()
                    backward(w, h * half, half)
                    if h == 0:
                        store(0).start()
        if cuts(window - 1) == 1:
            store(0).start()
        store(1).start()
        for w in range(window):
            for s in offsets:
                for k in range(2 * pieces(w)):
                    go(w, s, k).wait_send()
                for h in range(cuts(w)):
                    come(w, s, h).wait_send()
        for h in range(2):
            store(h).wait()

    def shards(targets, occupied, owners, cutoff_mask):
        count = targets.shape[2]
        slab = targets.shape[1]
        window = owners.shape[0]
        dma = pltpu.SemaphoreType.DMA
        vmem = pl.BlockSpec(memory_space=pltpu.VMEM)
        far = pl.BlockSpec(memory_space=pl.ANY)
        f32 = jnp.float32
        wide, tall = (2 * count, 6 * count), (6 * count, 2 * count)
        return pl.pallas_call(
            kernel,
            out_shape=jax.ShapeDtypeStruct(targets.shape, f32),
            in_specs=[far, vmem, pl.BlockSpec(memory_space=pltpu.SMEM)] + [far] * 5,
            out_specs=far,
            scratch_shapes=[
                pltpu.VMEM(targets.shape, f32),
                pltpu.VMEM(targets.shape, f32),
                pltpu.VMEM(cutoff_mask.shape, jnp.int32),
                pltpu.VMEM(wide, jnp.bfloat16), pltpu.VMEM(tall, jnp.bfloat16),
                pltpu.VMEM(wide, jnp.bfloat16), pltpu.VMEM(tall, jnp.bfloat16),
                pltpu.VMEM((window, slab, count, count), f32),
                pltpu.VMEM((bits, window, slab // 2, count, count), f32),
                pltpu.VMEM((window, slab, count, count), f32),
                pltpu.VMEM((window, 2, slab, count, count), f32),
                pltpu.VMEM((window, 2, count, slab, count), f32),
                pltpu.VMEM((window, 2, slab, count, count), f32),
                pltpu.VMEM((window, 2, count, slab, count), f32),
                pltpu.VMEM((slab, count, count), f32),
                dma((window, most)), dma((window, most)),
                dma((window, bits, most)), dma((window, bits, most)),
                dma((window, most)), dma((window, most)),
                dma((window, groups, 2 * most)), dma((window, groups, 2 * most)),
                dma((window, groups, 2)), dma((window, groups, 2)),
                dma((window, 2)), dma((6,)), dma((2,)),
            ],
            compiler_params=pltpu.CompilerParams(
                collective_id=0, has_side_effects=True, vmem_limit_bytes=56 * 1024 * 1024
            ),
            name="exchange",
        )(targets, occupied, owners, cutoff_mask, *[jnp.asarray(t) for t in tables(count)])

    return jax.shard_map(
        shards,
        mesh=mesh,
        in_specs=(
            P("band", "grid", None, None),
            P("band", "grid", None, None),
            P(),
            P(None, "grid", None),
        ),
        out_specs=P("band", "grid", None, None),
        check_vma=False,
    )
```
